256 devices in a mesh: ctx: 32 (over x, z), head: 8 (over y, core).
Axes of the slice: x: 4, y: 4, z: 8, core: 2. Of those that a mesh axis runs over, the one named last changes fastest.
Arguments:
- keys: bfloat16 [2, 262144, 8, 128], P(None, 'ctx', 'head'), may hold values from -6.5 to 6.5
- values: bfloat16 [2, 262144, 8, 128], P(None, 'ctx', 'head'), may hold values from -6 to 6
- queries: bfloat16 [2, 2048, 64, 128], P(None, 'ctx', 'head'), may hold values from -14 to 14
- keep_blocks: int32 [2, 8, 512], P(None, 'head'), may hold values from 0 to 2047, as said below
- block_owner: int32 [2, 8, 512], P(None, 'head'), may hold values from 0 to 31, as said below
Outputs:
- pooled_mass: float32 [2, 8, 262144], P(None, 'head', 'ctx')
- shared_mass: float32 [2, 262144], P(None, 'ctx')
- compact_keys: bfloat16 [2, 8, 65536, 128], P(None, 'head', 'ctx')
- compact_values: bfloat16 [2, 8, 65536, 128], P(None, 'head', 'ctx')
- kept_mass: bfloat16 [2, 8, 512], P(None, 'head', 'ctx')
The draws below stay inside these ranges and needn't reach their ends.
Inputs may be any that keep to these rules, and one draw needn't show every extreme that they name: `keep_blocks`: for each layer and KV head, 512 distinct block indices in increasing order; block b holds positions b * 128 to b * 128 + 127. Block 0 and block 2047 are always kept. `block_owner`: for each layer and KV head every owner receives exactly 16 kept blocks, and at most 2 kept blocks of one owner lie in the same ctx shard (block // 64); some shard reaches 2 with some owner.
All inputs are finite; a program needn't handle non-finite values.
Results may differ from the reference program's by a relative error of at most 0.001.
Values may be sent and summed in bfloat16 or wider, within the bound.
No kernel may reach another device: no remote copies, remote signals or barrier semaphores. Data moves between devices by JAX's collectives and lax.ppermute only.
A program may use at most 128 MiB of HBM per device.

```python
import math
import jax
import jax.numpy as jnp
from jax import lax

HD = 128
KVH = 8
QH = 64
GROUP = 8
WIN = 64
BLOCK = 128
POOL = 7
LAYERS = 2
SEQ = 262144
BLK_DEV = 64
NBLK = 2048
KEEP = 512
N_CTX = 32


def shared_parts(key):
    sub = jax.random.fold_in(key, 101)
    first = jax.random.fold_in(sub, 0)
    direction = 2.0 * jax.random.randint(first, (LAYERS, KVH, HD), 0, 2).astype(jnp.float32) - 1.0
    return direction


def draw_keys(key, part):
    direction = shared_parts(key)
    key = jax.random.fold_in(key, 1)
    first = jax.random.fold_in(key, 0)
    shape = (LAYERS, SEQ, KVH, HD)
    raw = jnp.clip(jax.random.normal(first, shape, jnp.float32), -4.0, 4.0)
    ramp = 1.1
    place = jnp.arange(SEQ, dtype=jnp.float32) / SEQ
    field = raw + ramp * place[None, :, None, None] * direction[:, None, :, :]
    return field.astype(jnp.bfloat16)


def draw_queries(key, part):
    direction = shared_parts(key)
    key = jax.random.fold_in(key, 2)
    first = jax.random.fold_in(key, 0)
    total_rows = N_CTX * WIN
    shape = (LAYERS, total_rows, QH, HD)
    raw = jnp.clip(jax.random.normal(first, shape, jnp.float32), -4.0, 4.0)
    lift = jnp.repeat(direction, QH // KVH, axis=1) / math.sqrt(HD)
    field = raw + lift[:, None, :, :]
    return field.astype(jnp.bfloat16)


def keep_plan(key):
    sub = jax.random.fold_in(key, 202)
    subkeys = jax.random.split(sub, LAYERS * KVH)

    def one_plan(single):
        first, second, third, fourth, fifth = jax.random.split(single, 5)
        blocks = jnp.arange(NBLK, dtype=jnp.int32)
        shard = blocks // BLK_DEV
        hot = jax.random.randint(third, (), 0, N_CTX)
        score = jax.random.randint(first, (NBLK,), 0, 64)
        score = score + jax.random.randint(second, (N_CTX,), 0, 128)[shard]
        score = score + jnp.where(shard == hot, 4096, 0) + jnp.where(shard == N_CTX - 1, 96, 0)
        score = score + jnp.where((blocks == 0) | (blocks == NBLK - 1), 8192, 0)
        distinct = score * NBLK + jax.random.permutation(fourth, NBLK).astype(jnp.int32)
        chosen = jnp.sort(lax.top_k(distinct, KEEP)[1]).astype(jnp.int32)
        owners = jax.random.permutation(fifth, N_CTX).astype(jnp.int32)[jnp.arange(KEEP, dtype=jnp.int32) % N_CTX]
        return (chosen, owners)
    chosen, owners = jax.vmap(one_plan)(subkeys)
    return (chosen.reshape(LAYERS, KVH, KEEP), owners.reshape(LAYERS, KVH, KEEP))


def draw_keep_blocks(key, part):
    chosen, owners = keep_plan(key)
    return chosen


def draw_block_owner(key, part):
    chosen, owners = keep_plan(key)
    return owners


def block_scale(key, shape, cuts, low, top_value):
    level, own = 1.0, jax.random.fold_in(key, 6)
    for position, parts in cuts:
        heights = jnp.exp(jax.random.uniform(jax.random.fold_in(own, position), (parts,), jnp.float32, low / len(cuts), top_value / len(cuts)))
        level = level * jnp.repeat(heights, shape[position] // parts).reshape([-1 if axis == position else 1 for axis in range(len(shape))])
    return level


def gaussian(key, extent, scale, most, cuts=(), held_as=jnp.bfloat16):
    entries = jax.random.normal(key, extent, jnp.float32) * scale
    if len(cuts) > 0:
        entries = block_scale(key, extent, cuts, -0.22, 0.18) * entries
    return jnp.clip(entries, min=-most, max=most).astype(held_as)


def setup_inputs(seed: int = 0) -> dict:
    arg_keys = jax.random.split(jax.random.key(seed), 6)
    return {
        "keys": draw_keys(jax.random.fold_in(arg_keys[5], 71), 0),
        "values": gaussian(arg_keys[1], (LAYERS, SEQ, KVH, HD), 1.0, 6.0, ((1, 32), (2, 8))),
        "queries": draw_queries(jax.random.fold_in(arg_keys[5], 71), 0),
        "keep_blocks": draw_keep_blocks(jax.random.fold_in(arg_keys[5], 71), 0),
        "block_owner": draw_block_owner(jax.random.fold_in(arg_keys[5], 71), 0),
    }


def layer_mass(window_layer, keys_layer):
    query_pos = jnp.repeat(SEQ - WIN + jnp.arange(WIN, dtype=jnp.int32), GROUP)
    key_pos = jnp.arange(SEQ, dtype=jnp.int32)
    visible = key_pos[None, :] <= query_pos[:, None]
    scale = HD ** -0.5

    def one_head(head_index):
        block = lax.dynamic_slice_in_dim(window_layer, head_index * GROUP, GROUP, axis=1).reshape(WIN * GROUP, HD)
        head_keys = lax.dynamic_index_in_dim(keys_layer, head_index, axis=1, keepdims=False)
        scores = jnp.dot(block, head_keys.T, preferred_element_type=jnp.float32) * scale
        scores = jnp.where(visible, scores, -1e30)
        peak = jnp.max(scores, axis=1, keepdims=True)
        expo = jnp.exp(scores - peak)
        total = jnp.sum(expo, axis=1, keepdims=True)
        return jnp.sum(expo / total, axis=0) * (SEQ / (WIN * GROUP))

    return lax.map(one_head, jnp.arange(KVH, dtype=jnp.int32))


def reference(keys, values, queries, keep_blocks, block_owner):
    half = (POOL - 1) // 2
    pooled_list, shared_list, key_list, value_list, kept_list = [], [], [], [], []
    for layer in range(LAYERS):
        window_layer = queries[layer, N_CTX * WIN - WIN:, :, :]
        mass = layer_mass(window_layer, keys[layer])
        padded = jnp.pad(mass, ((0, 0), (half, half)))
        pooled = padded[:, 0:SEQ]
        for shift in range(1, POOL):
            pooled = pooled + padded[:, shift:shift + SEQ]
        pooled = pooled / POOL
        pooled_list.append(pooled)
        shared_list.append(jnp.sum(pooled, axis=0) / KVH)
        block_mass = jnp.sum(pooled.reshape(KVH, NBLK, BLOCK), axis=2).astype(jnp.bfloat16)
        entry = jnp.arange(KEEP, dtype=jnp.int32)
        order = jnp.argsort(block_owner[layer] * KEEP + entry[None, :], axis=1)
        chosen = jnp.take_along_axis(keep_blocks[layer], order, axis=1)
        positions = (chosen[:, :, None] * BLOCK + jnp.arange(BLOCK, dtype=jnp.int32)[None, None, :]).reshape(KVH, KEEP * BLOCK)
        head_index = jnp.arange(KVH, dtype=jnp.int32)[:, None]
        key_list.append(keys[layer][positions, head_index, :])
        value_list.append(values[layer][positions, head_index, :])
        kept_list.append(jnp.take_along_axis(block_mass, chosen, axis=1))
    return (jnp.stack(pooled_list), jnp.stack(shared_list), jnp.stack(key_list), jnp.stack(value_list), jnp.stack(kept_list))
```

```python
import functools
import math
import jax
import jax.numpy as jnp
from jax import lax
from jax.experimental import pallas as pl
from jax.experimental.pallas import tpu as pltpu
from jax.sharding import PartitionSpec as P

KVH = 8
BLOCK = 128
POOL = 7
LANES = 128
TILE = 1024
NEG = -1e30
MIB = 1 << 20


def pack_kernel(index_ref, keys_ref, values_ref, after_ref, out_ref, sem):
    slots = out_ref.shape[0]
    layers = keys_ref.shape[0]

    def body(slot, carry):
        for layer in range(layers):
            block = index_ref[layer, slot]
            pltpu.make_async_copy(
                keys_ref.at[layer, block], out_ref.at[slot, 2 * layer], sem
            ).start()
            pltpu.make_async_copy(
                values_ref.at[layer, block], out_ref.at[slot, 2 * layer + 1], sem
            ).start()
        return carry

    lax.fori_loop(0, slots, body, 0)
    pltpu.make_async_copy(out_ref, out_ref, sem).wait()


def pack(index, keys, values, after):
    layers, slots = index.shape
    return pl.pallas_call(
        pack_kernel,
        out_shape=jax.ShapeDtypeStruct((slots, 2 * layers) + keys.shape[2:], keys.dtype),
        in_specs=[
            pl.BlockSpec(memory_space=pltpu.SMEM),
            pl.BlockSpec(memory_space=pl.ANY),
            pl.BlockSpec(memory_space=pl.ANY),
            pl.BlockSpec(memory_space=pl.ANY),
        ],
        out_specs=pl.BlockSpec(memory_space=pl.ANY),
        scratch_shapes=[pltpu.SemaphoreType.DMA],
        compiler_params=pltpu.CompilerParams(vmem_limit_bytes=48 * MIB),
        cost_estimate=pl.CostEstimate(flops=0, bytes_accessed=16 * MIB, transcendentals=0),
        name="pack",
    )(index, keys, values, after)


def unpack_kernel(index_ref, got_ref, keys_ref, values_ref, sems):
    layers, count = index_ref.shape

    def body(entry, carry):
        for layer in range(layers):
            slot = index_ref[layer, entry]
            pltpu.make_async_copy(
                got_ref.at[slot, 2 * layer], keys_ref.at[layer, entry], sems.at[0]
            ).start()
            pltpu.make_async_copy(
                got_ref.at[slot, 2 * layer + 1], values_ref.at[layer, entry], sems.at[1]
            ).start()
        return carry

    lax.fori_loop(0, count, body, 0)
    pltpu.make_async_copy(keys_ref, keys_ref, sems.at[0]).wait()
    pltpu.make_async_copy(values_ref, values_ref, sems.at[1]).wait()


def unpack(index, got):
    layers, count = index.shape
    out = jax.ShapeDtypeStruct((layers, count) + got.shape[2:], got.dtype)
    return pl.pallas_call(
        unpack_kernel,
        out_shape=(out, out),
        in_specs=[pl.BlockSpec(memory_space=pltpu.SMEM), pl.BlockSpec(memory_space=pl.ANY)],
        out_specs=(pl.BlockSpec(memory_space=pltpu.VMEM), pl.BlockSpec(memory_space=pltpu.VMEM)),
        scratch_shapes=[pltpu.SemaphoreType.DMA((2,))],
        compiler_params=pltpu.CompilerParams(vmem_limit_bytes=48 * MIB),
        cost_estimate=pl.CostEstimate(flops=0, bytes_accessed=4 * MIB, transcendentals=0),
        name="unpack",
    )(index, got)


def logits(limit_ref, query_ref, key_ref, group, scale):
    raw = lax.dot_general(
        query_ref[0], key_ref[0], (((1,), (1,)), ((), ())), preferred_element_type=jnp.float32
    )
    start = pl.program_id(1) * TILE
    row = lax.broadcasted_iota(jnp.int32, raw.shape, 0) // group
    column = lax.broadcasted_iota(jnp.int32, raw.shape, 1) + start
    return jnp.where(column <= row + limit_ref[0], raw * scale, NEG)


def stats_kernel(group, scale, limit_ref, query_ref, key_ref, peak_ref, total_ref, peaks, totals):
    tile = pl.program_id(1)

    @pl.when(tile == 0)
    def _():
        peaks[...] = jnp.full_like(peaks, NEG)
        totals[...] = jnp.zeros_like(totals)

    score = logits(limit_ref, query_ref, key_ref, group, scale)
    rows, width = score.shape
    parts = [score[:, c : c + LANES] for c in range(0, width, LANES)]
    old = peaks[...]
    new = functools.reduce(jnp.maximum, parts, old)
    total = totals[...] * jnp.exp2(old - new)
    for part in parts:
        total = total + jnp.exp2(part - new)
    peaks[...] = new
    totals[...] = total

    @pl.when(tile == pl.num_programs(1) - 1)
    def _():
        peak = jnp.max(new, axis=1, keepdims=True)
        peak_ref[0] = peak
        total_ref[0] = jnp.sum(total * jnp.exp2(new - peak), axis=1, keepdims=True)


def local_stats(limit, query, keys, group, scale):
    layers, rows, head_dim = query.shape
    tiles = keys.shape[1] // TILE
    out = jax.ShapeDtypeStruct((layers, rows, 1), jnp.float32)
    spec = pl.BlockSpec((1, rows, 1), lambda l, t: (l, 0, 0))
    return pl.pallas_call(
        functools.partial(stats_kernel, group, scale),
        out_shape=(out, out),
        grid=(layers, tiles),
        in_specs=[
            pl.BlockSpec(memory_space=pltpu.SMEM),
            pl.BlockSpec((1, rows, head_dim), lambda l, t: (l, 0, 0)),
            pl.BlockSpec((1, TILE, head_dim), lambda l, t: (l, t, 0)),
        ],
        out_specs=(spec, spec),
        scratch_shapes=[pltpu.VMEM((rows, LANES), jnp.float32)] * 2,
        compiler_params=pltpu.CompilerParams(vmem_limit_bytes=32 * MIB),
        cost_estimate=pl.CostEstimate(
            flops=2 * layers * rows * keys.shape[1] * head_dim,
            bytes_accessed=keys.size * 2,
            transcendentals=layers * rows * keys.shape[1],
        ),
        name="stats",
    )(limit, query, keys)


def mass_kernel(
    group, scale, shard_len, total_len, limit_ref, query_ref, key_ref, edge_ref, peak_ref, factor_ref,
    mass_ref, edge_mass_ref,
):
    score = logits(limit_ref, query_ref, key_ref, group, scale)
    weight = jnp.exp2(score - peak_ref[0]) * factor_ref[0]
    mass_ref[0] = jnp.sum(weight, axis=0, keepdims=True)

    @pl.when(pl.program_id(1) == 0)
    def _():
        raw = lax.dot_general(
            query_ref[0],
            edge_ref[0],
            (((1,), (1,)), ((), ())),
            preferred_element_type=jnp.float32,
        )
        side = raw.shape[1] // 2
        row = lax.broadcasted_iota(jnp.int32, raw.shape, 0) // group
        column = lax.broadcasted_iota(jnp.int32, raw.shape, 1)
        column = jnp.where(column < side, column - side, column - side + shard_len)
        start = limit_ref[1]
        inside = (column + start >= 0) & (column + start < total_len)
        inside = inside & (column <= row + limit_ref[0])
        weight = jnp.exp2(jnp.where(inside, raw * scale, NEG) - peak_ref[0]) * factor_ref[0]
        edge_mass_ref[0] = jnp.sum(weight, axis=0, keepdims=True)


def local_mass(limit, query, keys, edges, peak, factor, group, scale, total_len):
    layers, rows, head_dim = query.shape
    shard_len = keys.shape[1]
    tiles = shard_len // TILE
    column = pl.BlockSpec((1, rows, 1), lambda l, t: (l, 0, 0))
    return pl.pallas_call(
        functools.partial(mass_kernel, group, scale, shard_len, total_len),
        out_shape=(
            jax.ShapeDtypeStruct((layers, 1, shard_len), jnp.float32),
            jax.ShapeDtypeStruct((layers, 1, edges.shape[1]), jnp.float32),
        ),
        grid=(layers, tiles),
        in_specs=[
            pl.BlockSpec(memory_space=pltpu.SMEM),
            pl.BlockSpec((1, rows, head_dim), lambda l, t: (l, 0, 0)),
            pl.BlockSpec((1, TILE, head_dim), lambda l, t: (l, t, 0)),
            pl.BlockSpec((1, edges.shape[1], head_dim), lambda l, t: (l, 0, 0)),
            column,
            column,
        ],
        out_specs=(
            pl.BlockSpec((1, 1, TILE), lambda l, t: (l, 0, t)),
            pl.BlockSpec((1, 1, edges.shape[1]), lambda l, t: (l, 0, 0)),
        ),
        compiler_params=pltpu.CompilerParams(vmem_limit_bytes=32 * MIB),
        cost_estimate=pl.CostEstimate(
            flops=2 * layers * rows * shard_len * head_dim,
            bytes_accessed=keys.size * 2,
            transcendentals=layers * rows * shard_len,
        ),
        name="mass",
    )(limit, query, keys, edges, peak, factor)


def broadcast_plan(width, fan):
    rounds = []
    step = width
    while step > 1:
        split = min(fan, step)
        step //= split
        rounds.append((split, step))
    return rounds


def spread(x, axis):
    width = lax.axis_size(axis)
    place = lax.axis_index(axis)
    span = width
    for split, step in broadcast_plan(width, 4):
        holders = [i for i in range(width) if (i + 1) % span == 0]
        held = (place + 1) % span == 0
        got = x
        moved = [
            lax.ppermute(x, axis, [(i, i - turn * step) for i in holders])
            for turn in range(1, split)
        ]
        merged = functools.reduce(jnp.add, moved)
        x = jnp.where(held, got, merged)
        span = step
    return x


def partners(axis, bit):
    return [(i, i ^ bit) for i in range(lax.axis_size(axis))]


def merge_stats(peak, total, axis):
    bit = 1
    both = jnp.stack([peak, total])
    while bit < lax.axis_size(axis):
        other = lax.ppermute(both, axis, partners(axis, bit))
        top = jnp.maximum(both[0], other[0])
        both = jnp.stack(
            [top, both[1] * jnp.exp2(both[0] - top) + other[1] * jnp.exp2(other[0] - top)]
        )
        bit *= 2
    return both[0], both[1]


def total_over(x, axis):
    bit = 1
    while bit < lax.axis_size(axis):
        x = x + lax.ppermute(x, axis, partners(axis, bit))
        bit *= 2
    return x


def per_device(keys, values, queries, keep_blocks, block_owner):
    width = lax.axis_size("ctx")
    position = lax.axis_index("ctx")
    layers, shard_len, heads_here, head_dim = keys.shape
    window = queries.shape[1]
    group = queries.shape[2] // heads_here
    total_len = shard_len * width
    rows = window * group
    blocks_here = shard_len // BLOCK
    keep_count = keep_blocks.shape[2]
    keep_share = keep_count // width
    capacity = (blocks_here + width - 1) // width
    keys = keys.reshape(layers, shard_len, head_dim)
    values = values.reshape(layers, shard_len, head_dim)
    kept = keep_blocks[:, 0]
    owner = block_owner[:, 0]
    source = kept // blocks_here
    entry = jnp.arange(keep_count, dtype=jnp.int32)
    earlier = entry[None, :] < entry[:, None]
    same_owner = owner[:, :, None] == owner[:, None, :]
    same_source = source[:, :, None] == source[:, None, :]
    owner_rank = jnp.sum(same_owner & earlier, axis=-1)
    pair_rank = jnp.sum(same_owner & same_source & earlier, axis=-1)
    slot = owner * capacity + pair_rank
    send_hit = (source == position)[..., None] & (
        slot[..., None] == jnp.arange(width * capacity, dtype=jnp.int32)
    )
    send_index = jnp.sum(jnp.where(send_hit, (kept % blocks_here)[..., None], 0), axis=1)
    recv_hit = (owner == position)[..., None] & (
        owner_rank[..., None] == jnp.arange(keep_share, dtype=jnp.int32)
    )
    recv_index = jnp.sum(jnp.where(recv_hit, (source * capacity + pair_rank)[..., None], 0), axis=1)

    side = 8
    half = (POOL - 1) // 2
    forward = [(i, i + 1) for i in range(width - 1)]
    backward = [(i + 1, i) for i in range(width - 1)]
    low = lax.ppermute(keys[:, shard_len - side :], "ctx", forward)
    high = lax.ppermute(keys[:, :side], "ctx", backward)
    edges = jnp.concatenate([low, high], axis=1)
    windowed = spread(queries, "ctx").reshape(layers, rows, head_dim)
    start = position * shard_len
    limit = jnp.stack([total_len - window - start, start])
    scale = head_dim**-0.5 * math.log2(math.e)
    peak, total = local_stats(limit, windowed, keys, group, scale)
    peak, total = merge_stats(peak.reshape(layers, rows), total.reshape(layers, rows), "ctx")

    blocked = (layers, blocks_here, BLOCK, head_dim)
    parcels = pack(send_index, keys.reshape(blocked), values.reshape(blocked), total)
    got = lax.all_to_all(parcels, "ctx", split_axis=0, concat_axis=0, tiled=True)

    factor = (total_len / rows) / total
    mass, edge_mass = local_mass(
        limit, windowed, keys, edges, peak[..., None], factor[..., None], group, scale, total_len
    )
    padded = jnp.concatenate(
        [edge_mass[:, 0, side - half : side], mass[:, 0], edge_mass[:, 0, side : side + half]],
        axis=1,
    )
    pooled = padded[:, 0:shard_len]
    for shift in range(1, POOL):
        pooled = pooled + padded[:, shift : shift + shard_len]
    pooled = pooled / POOL
    shared = total_over(pooled, "head") / KVH
    block_mass = jnp.sum(pooled.reshape(layers, blocks_here, BLOCK), axis=2).astype(jnp.bfloat16)
    sent_mass = jnp.take_along_axis(block_mass, send_index, axis=1)
    got_mass = lax.all_to_all(sent_mass, "ctx", split_axis=1, concat_axis=1, tiled=True)
    kept_mass = jnp.take_along_axis(got_mass, recv_index, axis=1)

    compact_keys, compact_values = unpack(recv_index, got)
    share = (layers, heads_here, keep_share * BLOCK, head_dim)
    return (
        pooled[:, None],
        shared,
        compact_keys.reshape(share),
        compact_values.reshape(share),
        kept_mass[:, None],
    )


def solution(mesh):
    in_specs = (
        P(None, "ctx", "head", None),
        P(None, "ctx", "head", None),
        P(None, "ctx", "head", None),
        P(None, "head", None),
        P(None, "head", None),
    )
    out_specs = (
        P(None, "head", "ctx"),
        P(None, "ctx"),
        P(None, "head", "ctx", None),
        P(None, "head", "ctx", None),
        P(None, "head", "ctx"),
    )
    return jax.shard_map(
        per_device, mesh=mesh, in_specs=in_specs, out_specs=out_specs, check_vma=False
    )
```

```python
import functools
import math
import jax
import jax.numpy as jnp
from jax import lax
from jax.experimental import pallas as pl
from jax.experimental.pallas import tpu as pltpu
from jax.sharding import PartitionSpec as P

KVH = 8
BLOCK = 128
POOL = 7
LANES = 128
TILE = 1024
NEG = -1e30
MIB = 1 << 20


def pack_kernel(layer, parts, index_ref, keys_ref, values_ref, *rest):
    out_ref, done_ref, hold, sems, out_sem = rest[-5:]
    done_ref[...] = jnp.zeros_like(done_ref)
    share = hold.shape[0] // parts
    stores = []

    for part in range(parts):

        def body(slot, carry):
            block = index_ref[layer, slot]
            pltpu.make_async_copy(keys_ref.at[layer, block], hold.at[slot, 0], sems.at[part]).start()
            pltpu.make_async_copy(values_ref.at[layer, block], hold.at[slot, 1], sems.at[part]).start()
            return carry

        lax.fori_loop(part * share, (part + 1) * share, body, 0, unroll=8)
    for part in range(parts):
        some = hold.at[pl.ds(part * share, share)]
        pltpu.make_async_copy(some, some, sems.at[part]).wait()
        store = pltpu.make_async_copy(
            some, out_ref.at[pl.ds(part * share, share), pl.ds(2 * layer, 2)], out_sem.at[part]
        )
        store.start()
        stores.append(store)
    for store in stores:
        store.wait()


def pack(index, keys, values):
    layers, slots = index.shape
    parts = 4
    out = jax.ShapeDtypeStruct((slots, 2 * layers) + keys.shape[2:], keys.dtype)
    done = jax.ShapeDtypeStruct((8, LANES), jnp.float32)
    parcels, stages = None, []
    for layer in range(layers):
        first = not stages
        parcels, stage = pl.pallas_call(
            functools.partial(pack_kernel, layer, parts),
            out_shape=(out, done),
            in_specs=[pl.BlockSpec(memory_space=pltpu.SMEM)]
            + [pl.BlockSpec(memory_space=pl.ANY)] * (2 if first else 3),
            out_specs=(pl.BlockSpec(memory_space=pl.ANY), pl.BlockSpec(memory_space=pltpu.VMEM)),
            scratch_shapes=[
                pltpu.VMEM((slots, 2) + keys.shape[2:], keys.dtype),
                pltpu.SemaphoreType.DMA((parts,)),
                pltpu.SemaphoreType.DMA((parts,)),
            ],
            input_output_aliases={} if first else {3: 0},
            compiler_params=pltpu.CompilerParams(vmem_limit_bytes=60 * MIB),
            cost_estimate=pl.CostEstimate(flops=0, bytes_accessed=16 * MIB, transcendentals=0),
            name="pack",
        )(index, keys, values, *([] if first else [parcels]))
        stages.append(stage)
    return parcels, stages


def gate_kernel(*refs):
    pass


def gate(array, *after):
    return pl.pallas_call(
        gate_kernel,
        out_shape=jax.ShapeDtypeStruct(array.shape, array.dtype),
        in_specs=[pl.BlockSpec(memory_space=pl.ANY)] * (1 + len(after)),
        out_specs=pl.BlockSpec(memory_space=pl.ANY),
        input_output_aliases={0: 0},
        name="gate",
    )(array, *after)


def unpack_kernel(index_ref, got_ref, keys_ref, values_ref, sems):
    layers, count = index_ref.shape

    def body(entry, carry):
        for layer in range(layers):
            slot = index_ref[layer, entry]
            pltpu.make_async_copy(
                got_ref.at[slot, 2 * layer], keys_ref.at[layer, entry], sems.at[0]
            ).start()
            pltpu.make_async_copy(
                got_ref.at[slot, 2 * layer + 1], values_ref.at[layer, entry], sems.at[1]
            ).start()
        return carry

    lax.fori_loop(0, count, body, 0)
    pltpu.make_async_copy(keys_ref, keys_ref, sems.at[0]).wait()
    pltpu.make_async_copy(values_ref, values_ref, sems.at[1]).wait()


def unpack(index, got):
    layers, count = index.shape
    out = jax.ShapeDtypeStruct((layers, count) + got.shape[2:], got.dtype)
    return pl.pallas_call(
        unpack_kernel,
        out_shape=(out, out),
        in_specs=[pl.BlockSpec(memory_space=pltpu.SMEM), pl.BlockSpec(memory_space=pl.ANY)],
        out_specs=(pl.BlockSpec(memory_space=pltpu.VMEM), pl.BlockSpec(memory_space=pltpu.VMEM)),
        scratch_shapes=[pltpu.SemaphoreType.DMA((2,))],
        compiler_params=pltpu.CompilerParams(vmem_limit_bytes=60 * MIB),
        cost_estimate=pl.CostEstimate(flops=0, bytes_accessed=4 * MIB, transcendentals=0),
        name="unpack",
    )(index, got)


def logits(limit_ref, query_ref, key_ref, group, scale):
    raw = lax.dot_general(
        query_ref[0], key_ref[0], (((1,), (1,)), ((), ())), preferred_element_type=jnp.float32
    )
    start = pl.program_id(1) * TILE
    row = lax.broadcasted_iota(jnp.int32, raw.shape, 0) // group
    column = lax.broadcasted_iota(jnp.int32, raw.shape, 1) + start
    return jnp.where(column <= row + limit_ref[0], raw * scale, NEG)


def stats_kernel(group, scale, limit_ref, query_ref, key_ref, peak_ref, total_ref, peaks, totals):
    tile = pl.program_id(1)

    @pl.when(tile == 0)
    def _():
        peaks[...] = jnp.full_like(peaks, NEG)
        totals[...] = jnp.zeros_like(totals)

    score = logits(limit_ref, query_ref, key_ref, group, scale)
    rows, width = score.shape
    parts = [score[:, c : c + LANES] for c in range(0, width, LANES)]
    old = peaks[...]
    new = functools.reduce(jnp.maximum, parts, old)
    total = totals[...] * jnp.exp2(old - new)
    for part in parts:
        total = total + jnp.exp2(part - new)
    peaks[...] = new
    totals[...] = total

    @pl.when(tile == pl.num_programs(1) - 1)
    def _():
        peak = jnp.max(new, axis=1, keepdims=True)
        peak_ref[0] = peak
        total_ref[0] = jnp.sum(total * jnp.exp2(new - peak), axis=1, keepdims=True)


def local_stats(limit, query, keys, group, scale):
    layers, rows, head_dim = query.shape
    tiles = keys.shape[1] // TILE
    out = jax.ShapeDtypeStruct((layers, rows, 1), jnp.float32)
    spec = pl.BlockSpec((1, rows, 1), lambda l, t: (l, 0, 0))
    return pl.pallas_call(
        functools.partial(stats_kernel, group, scale),
        out_shape=(out, out),
        grid=(layers, tiles),
        in_specs=[
            pl.BlockSpec(memory_space=pltpu.SMEM),
            pl.BlockSpec((1, rows, head_dim), lambda l, t: (l, 0, 0)),
            pl.BlockSpec((1, TILE, head_dim), lambda l, t: (l, t, 0)),
        ],
        out_specs=(spec, spec),
        scratch_shapes=[pltpu.VMEM((rows, LANES), jnp.float32)] * 2,
        compiler_params=pltpu.CompilerParams(vmem_limit_bytes=60 * MIB),
        cost_estimate=pl.CostEstimate(
            flops=2 * layers * rows * keys.shape[1] * head_dim,
            bytes_accessed=keys.size * 2,
            transcendentals=layers * rows * keys.shape[1],
        ),
        name="stats",
    )(limit, query, keys)


def mass_kernel(
    group, scale, shard_len, total_len, limit_ref, query_ref, key_ref, edge_ref, peak_ref, factor_ref,
    mass_ref, edge_mass_ref,
):
    score = logits(limit_ref, query_ref, key_ref, group, scale)
    weight = jnp.exp2(score - peak_ref[0]) * factor_ref[0]
    mass_ref[0] = jnp.sum(weight, axis=0, keepdims=True)

    @pl.when(pl.program_id(1) == 0)
    def _():
        raw = lax.dot_general(
            query_ref[0],
            edge_ref[0],
            (((1,), (1,)), ((), ())),
            preferred_element_type=jnp.float32,
        )
        side = raw.shape[1] // 2
        row = lax.broadcasted_iota(jnp.int32, raw.shape, 0) // group
        column = lax.broadcasted_iota(jnp.int32, raw.shape, 1)
        column = jnp.where(column < side, column - side, column - side + shard_len)
        start = limit_ref[1]
        inside = (column + start >= 0) & (column + start < total_len)
        inside = inside & (column <= row + limit_ref[0])
        weight = jnp.exp2(jnp.where(inside, raw * scale, NEG) - peak_ref[0]) * factor_ref[0]
        edge_mass_ref[0] = jnp.sum(weight, axis=0, keepdims=True)


def local_mass(limit, query, keys, edges, peak, factor, group, scale, total_len):
    layers, rows, head_dim = query.shape
    shard_len = keys.shape[1]
    tiles = shard_len // TILE
    column = pl.BlockSpec((1, rows, 1), lambda l, t: (l, 0, 0))
    return pl.pallas_call(
        functools.partial(mass_kernel, group, scale, shard_len, total_len),
        out_shape=(
            jax.ShapeDtypeStruct((layers, 1, shard_len), jnp.float32),
            jax.ShapeDtypeStruct((layers, 1, edges.shape[1]), jnp.float32),
        ),
        grid=(layers, tiles),
        in_specs=[
            pl.BlockSpec(memory_space=pltpu.SMEM),
            pl.BlockSpec((1, rows, head_dim), lambda l, t: (l, 0, 0)),
            pl.BlockSpec((1, TILE, head_dim), lambda l, t: (l, t, 0)),
            pl.BlockSpec((1, edges.shape[1], head_dim), lambda l, t: (l, 0, 0)),
            column,
            column,
        ],
        out_specs=(
            pl.BlockSpec((1, 1, TILE), lambda l, t: (l, 0, t)),
            pl.BlockSpec((1, 1, edges.shape[1]), lambda l, t: (l, 0, 0)),
        ),
        compiler_params=pltpu.CompilerParams(vmem_limit_bytes=60 * MIB),
        cost_estimate=pl.CostEstimate(
            flops=2 * layers * rows * shard_len * head_dim,
            bytes_accessed=keys.size * 2,
            transcendentals=layers * rows * shard_len,
        ),
        name="mass",
    )(limit, query, keys, edges, peak, factor)


def spread_rounds(wide, deep, root):
    held, rounds = [root], []
    while len(held) < wide * deep:
        used, taken, moves = set(), set(held), []
        for far in range(1, max(wide, deep) // 2 + 1):
            for x, z in held:
                for sx, sz in ((1, 0), (-1, 0), (0, 1), (0, -1)):
                    hops = 3 if sz and not rounds else far
                    if hops > (wide if sx else deep) // 2 or (not rounds and far > 1):
                        continue
                    path = [((x + sx * k) % wide, (z + sz * k) % deep, sx, sz) for k in range(hops)]
                    target = ((x + sx * hops) % wide, (z + sz * hops) % deep)
                    if target in taken or any(link in used for link in path):
                        continue
                    used.update(path)
                    taken.add(target)
                    moves.append((x * deep + z, target[0] * deep + target[1]))
        rounds.append(moves)
        held = sorted(taken)
    return rounds


def spread(x, axis, between):
    width = lax.axis_size(axis)
    place = lax.axis_index(axis)
    deep = 8 if width % 8 == 0 else width
    wide = width // deep
    held = [width - 1]
    for index, moves in enumerate(spread_rounds(wide, deep, (wide - 1, deep - 1))):
        perms = []
        for source, target in moves:
            free = [perm for perm in perms if source not in [pair[0] for pair in perm]]
            if free:
                free[0].append((source, target))
            else:
                perms.append([(source, target)])
        moved = functools.reduce(jnp.add, [lax.ppermute(x, axis, perm) for perm in perms])
        mine = functools.reduce(jnp.logical_or, [place == one for one in held])
        x = jnp.where(mine, x, moved)
        held = held + [target for _, target in moves]
        if index < len(between):
            x = gate(x, between[index])
    return x


def partners(axis, bit):
    return [(i, i ^ bit) for i in range(lax.axis_size(axis))]


def merge_stats(peak, total, axis):
    both = jnp.concatenate([peak, total] * 4, axis=0)
    every = lax.all_gather(both, axis, axis=0, tiled=False)
    layers = peak.shape[0]
    peaks, totals = every[:, :layers], every[:, layers : 2 * layers]
    top = jnp.max(peaks, axis=0)
    return top, jnp.sum(totals * jnp.exp2(peaks - top), axis=0)


def total_over(x, axis):
    bit = 1
    while bit < lax.axis_size(axis):
        x = x + lax.ppermute(x, axis, partners(axis, bit))
        bit *= 2
    return x


def per_device(keys, values, queries, keep_blocks, block_owner):
    width = lax.axis_size("ctx")
    position = lax.axis_index("ctx")
    layers, shard_len, heads_here, head_dim = keys.shape
    window = queries.shape[1]
    group = queries.shape[2] // heads_here
    total_len = shard_len * width
    rows = window * group
    blocks_here = shard_len // BLOCK
    keep_count = keep_blocks.shape[2]
    keep_share = keep_count // width
    capacity = (blocks_here + width - 1) // width
    keys = keys.reshape(layers, shard_len, head_dim)
    values = values.reshape(layers, shard_len, head_dim)
    kept = keep_blocks[:, 0]
    owner = block_owner[:, 0]
    source = kept // blocks_here
    entry = jnp.arange(keep_count, dtype=jnp.int32)
    earlier = entry[None, :] < entry[:, None]
    same_owner = owner[:, :, None] == owner[:, None, :]
    same_source = source[:, :, None] == source[:, None, :]
    owner_rank = jnp.sum(same_owner & earlier, axis=-1)
    pair_rank = jnp.sum(same_owner & same_source & earlier, axis=-1)
    slot = owner * capacity + pair_rank
    send_hit = (source == position)[..., None] & (
        slot[..., None] == jnp.arange(width * capacity, dtype=jnp.int32)
    )
    send_index = jnp.sum(jnp.where(send_hit, (kept % blocks_here)[..., None], 0), axis=1)
    recv_hit = (owner == position)[..., None] & (
        owner_rank[..., None] == jnp.arange(keep_share, dtype=jnp.int32)
    )
    recv_index = jnp.sum(jnp.where(recv_hit, (source * capacity + pair_rank)[..., None], 0), axis=1)

    side = 8
    half = (POOL - 1) // 2
    forward = [(i, i + 1) for i in range(width - 1)]
    backward = [(i + 1, i) for i in range(width - 1)]
    low = lax.ppermute(keys[:, shard_len - side :], "ctx", forward)
    high = lax.ppermute(keys[:, :side], "ctx", backward)
    edges = jnp.concatenate([low, high], axis=1)
    blocked = (layers, blocks_here, BLOCK, head_dim)
    parcels, stages = pack(send_index, keys.reshape(blocked), values.reshape(blocked))
    windowed = spread(queries, "ctx", stages).reshape(layers, rows, head_dim)
    start = position * shard_len
    limit = jnp.stack([total_len - window - start, start])
    scale = head_dim**-0.5 * math.log2(math.e)
    parcels = gate(parcels, windowed, edges)
    got = lax.all_to_all(parcels, "ctx", split_axis=0, concat_axis=0, tiled=True)

    peak, total = local_stats(limit, windowed, keys, group, scale)
    peak, total = merge_stats(peak.reshape(layers, rows), total.reshape(layers, rows), "ctx")
    factor = (total_len / rows) / total
    mass, edge_mass = local_mass(
        limit, windowed, keys, edges, peak[..., None], factor[..., None], group, scale, total_len
    )
    padded = jnp.concatenate(
        [edge_mass[:, 0, side - half : side], mass[:, 0], edge_mass[:, 0, side : side + half]],
        axis=1,
    )
    pooled = padded[:, 0:shard_len]
    for shift in range(1, POOL):
        pooled = pooled + padded[:, shift : shift + shard_len]
    pooled = pooled / POOL
    shared = total_over(pooled, "head") / KVH
    block_mass = jnp.sum(pooled.reshape(layers, blocks_here, BLOCK), axis=2).astype(jnp.bfloat16)
    sent_mass = jnp.take_along_axis(block_mass, send_index, axis=1)
    got, sent_mass = lax.optimization_barrier((got, sent_mass))
    got_mass = lax.all_to_all(sent_mass, "ctx", split_axis=1, concat_axis=1, tiled=True)
    kept_mass = jnp.take_along_axis(got_mass, recv_index, axis=1)

    compact_keys, compact_values = unpack(recv_index, got)
    share = (layers, heads_here, keep_share * BLOCK, head_dim)
    return (
        pooled[:, None],
        shared,
        compact_keys.reshape(share),
        compact_values.reshape(share),
        kept_mass[:, None],
    )


def solution(mesh):
    in_specs = (
        P(None, "ctx", "head", None),
        P(None, "ctx", "head", None),
        P(None, "ctx", "head", None),
        P(None, "head", None),
        P(None, "head", None),
    )
    out_specs = (
        P(None, "head", "ctx"),
        P(None, "ctx"),
        P(None, "head", "ctx", None),
        P(None, "head", "ctx", None),
        P(None, "head", "ctx"),
    )
    return jax.shard_map(
        per_device, mesh=mesh, in_specs=in_specs, out_specs=out_specs, check_vma=False
    )
```

```python
import functools
import math
import jax
import jax.numpy as jnp
from jax import lax
from jax.experimental import pallas as pl
from jax.experimental.pallas import tpu as pltpu
from jax.sharding import PartitionSpec as P

KVH = 8
BLOCK = 128
POOL = 7
LANES = 128
TILE = 1024
NEG = -1e30
MIB = 1 << 20


def pack_kernel(first, parts, index_ref, keys_ref, values_ref, *rest):
    out_ref = rest[-1]
    step = first + pl.program_id(0)
    layer, part = step // parts, step % parts
    share = out_ref.shape[0]
    for slot in range(share):
        block = index_ref[layer, part * share + slot]
        out_ref[slot, 0] = keys_ref[0, block]
        out_ref[slot, 1] = values_ref[0, block]


def pack(index, keys, values, first, count, after, parcels=None):
    layers, slots = index.shape
    parts = 2
    whole = pl.BlockSpec((1,) + keys.shape[1:], lambda i: ((first + i) // parts, 0, 0, 0))
    others = [after] if parcels is None else [after, parcels]
    return pl.pallas_call(
        functools.partial(pack_kernel, first, parts),
        out_shape=jax.ShapeDtypeStruct((slots, 2 * layers) + keys.shape[2:], keys.dtype),
        grid=(count,),
        in_specs=[pl.BlockSpec(memory_space=pltpu.SMEM), whole, whole]
        + [pl.BlockSpec(memory_space=pl.ANY)] * len(others),
        out_specs=pl.BlockSpec(
            (slots // parts, 2) + keys.shape[2:],
            lambda i: ((first + i) % parts, (first + i) // parts, 0, 0),
        ),
        input_output_aliases={} if parcels is None else {4: 0},
        compiler_params=pltpu.CompilerParams(vmem_limit_bytes=60 * MIB),
        cost_estimate=pl.CostEstimate(flops=0, bytes_accessed=8 * MIB, transcendentals=0),
        name="pack",
    )(index, keys, values, *others)


def gate_kernel(*refs):
    pass


def gate(array, *after):
    return pl.pallas_call(
        gate_kernel,
        out_shape=jax.ShapeDtypeStruct(array.shape, array.dtype),
        in_specs=[pl.BlockSpec(memory_space=pl.ANY)] * (1 + len(after)),
        out_specs=pl.BlockSpec(memory_space=pl.ANY),
        input_output_aliases={0: 0},
        name="gate",
    )(array, *after)


def unpack_kernel(index_ref, got_ref, keys_ref, values_ref, sems):
    layers, count = index_ref.shape

    def body(entry, carry):
        for layer in range(layers):
            slot = index_ref[layer, entry]
            pltpu.make_async_copy(
                got_ref.at[slot, 2 * layer], keys_ref.at[layer, entry], sems.at[0]
            ).start()
            pltpu.make_async_copy(
                got_ref.at[slot, 2 * layer + 1], values_ref.at[layer, entry], sems.at[1]
            ).start()
        return carry

    lax.fori_loop(0, count, body, 0)
    pltpu.make_async_copy(keys_ref, keys_ref, sems.at[0]).wait()
    pltpu.make_async_copy(values_ref, values_ref, sems.at[1]).wait()


def unpack(index, got):
    layers, count = index.shape
    out = jax.ShapeDtypeStruct((layers, count) + got.shape[2:], got.dtype)
    return pl.pallas_call(
        unpack_kernel,
        out_shape=(out, out),
        in_specs=[pl.BlockSpec(memory_space=pltpu.SMEM), pl.BlockSpec(memory_space=pl.ANY)],
        out_specs=(pl.BlockSpec(memory_space=pltpu.VMEM), pl.BlockSpec(memory_space=pltpu.VMEM)),
        scratch_shapes=[pltpu.SemaphoreType.DMA((2,))],
        compiler_params=pltpu.CompilerParams(vmem_limit_bytes=60 * MIB),
        cost_estimate=pl.CostEstimate(flops=0, bytes_accessed=4 * MIB, transcendentals=0),
        name="unpack",
    )(index, got)


def logits(limit_ref, query_ref, key_ref, group, scale):
    raw = lax.dot_general(
        query_ref[0], key_ref[0], (((1,), (1,)), ((), ())), preferred_element_type=jnp.float32
    )
    start = pl.program_id(1) * TILE
    row = lax.broadcasted_iota(jnp.int32, raw.shape, 0) // group
    column = lax.broadcasted_iota(jnp.int32, raw.shape, 1) + start
    return jnp.where(column <= row + limit_ref[0], raw * scale, NEG)


def stats_kernel(group, scale, limit_ref, query_ref, key_ref, peak_ref, total_ref, peaks, totals):
    tile = pl.program_id(1)

    @pl.when(tile == 0)
    def _():
        peaks[...] = jnp.full_like(peaks, NEG)
        totals[...] = jnp.zeros_like(totals)

    score = logits(limit_ref, query_ref, key_ref, group, scale)
    rows, width = score.shape
    parts = [score[:, c : c + LANES] for c in range(0, width, LANES)]
    old = peaks[...]
    new = functools.reduce(jnp.maximum, parts, old)
    total = totals[...] * jnp.exp2(old - new)
    for part in parts:
        total = total + jnp.exp2(part - new)
    peaks[...] = new
    totals[...] = total

    @pl.when(tile == pl.num_programs(1) - 1)
    def _():
        peak = jnp.max(new, axis=1, keepdims=True)
        peak_ref[0] = peak
        total_ref[0] = jnp.sum(total * jnp.exp2(new - peak), axis=1, keepdims=True)


def local_stats(limit, query, keys, group, scale):
    layers, rows, head_dim = query.shape
    tiles = keys.shape[1] // TILE
    out = jax.ShapeDtypeStruct((layers, rows, 1), jnp.float32)
    spec = pl.BlockSpec((1, rows, 1), lambda l, t: (l, 0, 0))
    return pl.pallas_call(
        functools.partial(stats_kernel, group, scale),
        out_shape=(out, out),
        grid=(layers, tiles),
        in_specs=[
            pl.BlockSpec(memory_space=pltpu.SMEM),
            pl.BlockSpec((1, rows, head_dim), lambda l, t: (l, 0, 0)),
            pl.BlockSpec((1, TILE, head_dim), lambda l, t: (l, t, 0)),
        ],
        out_specs=(spec, spec),
        scratch_shapes=[pltpu.VMEM((rows, LANES), jnp.float32)] * 2,
        compiler_params=pltpu.CompilerParams(vmem_limit_bytes=60 * MIB),
        cost_estimate=pl.CostEstimate(
            flops=2 * layers * rows * keys.shape[1] * head_dim,
            bytes_accessed=keys.size * 2,
            transcendentals=layers * rows * keys.shape[1],
        ),
        name="stats",
    )(limit, query, keys)


def mass_kernel(
    group, scale, shard_len, total_len, limit_ref, query_ref, key_ref, edge_ref, peak_ref, factor_ref,
    mass_ref, edge_mass_ref,
):
    score = logits(limit_ref, query_ref, key_ref, group, scale)
    weight = jnp.exp2(score - peak_ref[0]) * factor_ref[0]
    mass_ref[0] = jnp.sum(weight, axis=0, keepdims=True)

    @pl.when(pl.program_id(1) == 0)
    def _():
        raw = lax.dot_general(
            query_ref[0],
            edge_ref[0],
            (((1,), (1,)), ((), ())),
            preferred_element_type=jnp.float32,
        )
        side = raw.shape[1] // 2
        row = lax.broadcasted_iota(jnp.int32, raw.shape, 0) // group
        column = lax.broadcasted_iota(jnp.int32, raw.shape, 1)
        column = jnp.where(column < side, column - side, column - side + shard_len)
        start = limit_ref[1]
        inside = (column + start >= 0) & (column + start < total_len)
        inside = inside & (column <= row + limit_ref[0])
        weight = jnp.exp2(jnp.where(inside, raw * scale, NEG) - peak_ref[0]) * factor_ref[0]
        edge_mass_ref[0] = jnp.sum(weight, axis=0, keepdims=True)


def local_mass(limit, query, keys, edges, peak, factor, group, scale, total_len):
    layers, rows, head_dim = query.shape
    shard_len = keys.shape[1]
    tiles = shard_len // TILE
    column = pl.BlockSpec((1, rows, 1), lambda l, t: (l, 0, 0))
    return pl.pallas_call(
        functools.partial(mass_kernel, group, scale, shard_len, total_len),
        out_shape=(
            jax.ShapeDtypeStruct((layers, 1, shard_len), jnp.float32),
            jax.ShapeDtypeStruct((layers, 1, edges.shape[1]), jnp.float32),
        ),
        grid=(layers, tiles),
        in_specs=[
            pl.BlockSpec(memory_space=pltpu.SMEM),
            pl.BlockSpec((1, rows, head_dim), lambda l, t: (l, 0, 0)),
            pl.BlockSpec((1, TILE, head_dim), lambda l, t: (l, t, 0)),
            pl.BlockSpec((1, edges.shape[1], head_dim), lambda l, t: (l, 0, 0)),
            column,
            column,
        ],
        out_specs=(
            pl.BlockSpec((1, 1, TILE), lambda l, t: (l, 0, t)),
            pl.BlockSpec((1, 1, edges.shape[1]), lambda l, t: (l, 0, 0)),
        ),
        compiler_params=pltpu.CompilerParams(vmem_limit_bytes=60 * MIB),
        cost_estimate=pl.CostEstimate(
            flops=2 * layers * rows * shard_len * head_dim,
            bytes_accessed=keys.size * 2,
            transcendentals=layers * rows * shard_len,
        ),
        name="mass",
    )(limit, query, keys, edges, peak, factor)


def grid_of(axis):
    width = lax.axis_size(axis)
    deep = 8 if width % 8 == 0 else width
    return width // deep, deep


def spread(x, axis, works):
    wide, deep = grid_of(axis)
    place = lax.axis_index(axis)
    across, along = place // deep, place % deep
    last = wide * deep - 1
    pieces = x.reshape((wide, -1) + x.shape[2:])
    moved = [
        lax.ppermute(pieces[k], axis, [(last, k * deep + deep - 1)]) for k in range(wide - 1)
    ]
    piece = jnp.where(place == last, pieces[wide - 1], functools.reduce(jnp.add, moved))
    held, result = [deep - 1], None
    for work, steps in zip(works, (range(2, deep, 2), (1,))):
        moved = [
            lax.ppermute(
                piece,
                axis,
                [(k * deep + z, k * deep + (z + dz) % deep) for k in range(wide) for z in held],
            )
            for dz in steps
        ]
        result = work(piece, result)
        mine = functools.reduce(jnp.logical_or, [along == z for z in held])
        piece = jnp.where(mine, piece, functools.reduce(jnp.add, moved))
        piece = gate(piece, result)
        held = held + [(z + dz) % deep for z in held for dz in steps]
    moved = [piece] + [
        lax.ppermute(
            piece,
            axis,
            [(k * deep + z, (k + dx) % wide * deep + z) for k in range(wide) for z in range(deep)],
        )
        for dx in range(1, wide)
    ]
    whole = [lax.select_n((across - k) % wide, *moved) for k in range(wide)]
    return jnp.stack(whole).reshape(x.shape), result, moved[1:]


def partners(axis, bit):
    return [(i, i ^ bit) for i in range(lax.axis_size(axis))]


def merge_stats(peak, total, ends, axis):
    layers, rows = peak.shape
    ends = ends.astype(jnp.float32).reshape(2, -1, rows)
    both = [peak, total, ends[0], ends[1]]
    used = sum(part.shape[0] for part in both)
    both = jnp.concatenate(both + [jnp.zeros((16 - used, rows), jnp.float32)], axis=0)
    every = lax.all_gather(both, axis, axis=0, tiled=False)
    peaks, totals = every[:, :layers], every[:, layers : 2 * layers]
    top = jnp.max(peaks, axis=0)
    total = jnp.sum(totals * jnp.exp2(peaks - top), axis=0)
    place, width = lax.axis_index(axis), lax.axis_size(axis)
    count = ends.shape[1]
    below = lax.dynamic_index_in_dim(every, jnp.maximum(place - 1, 0), 0, keepdims=False)
    above = lax.dynamic_index_in_dim(every, jnp.minimum(place + 1, width - 1), 0, keepdims=False)
    first = 2 * layers
    return top, total, below[first : first + count], above[first + count : first + 2 * count]


def total_over(x, axis):
    bit = 1
    while bit < lax.axis_size(axis):
        x = x + lax.ppermute(x, axis, partners(axis, bit))
        bit *= 2
    return x


def per_device(keys, values, queries, keep_blocks, block_owner):
    width = lax.axis_size("ctx")
    position = lax.axis_index("ctx")
    layers, shard_len, heads_here, head_dim = keys.shape
    window = queries.shape[1]
    group = queries.shape[2] // heads_here
    total_len = shard_len * width
    rows = window * group
    blocks_here = shard_len // BLOCK
    keep_count = keep_blocks.shape[2]
    keep_share = keep_count // width
    capacity = 2
    keys = keys.reshape(layers, shard_len, head_dim)
    values = values.reshape(layers, shard_len, head_dim)
    kept, owner = keep_blocks[:, 0], block_owner[:, 0]
    offset = (kept - position * blocks_here)[..., None]
    to_owner = (offset >= 0) & (offset < blocks_here)
    to_owner = to_owner & (owner[..., None] == jnp.arange(width, dtype=jnp.int32))
    lowest = jnp.min(jnp.where(to_owner, offset, blocks_here), axis=1)
    highest = jnp.max(jnp.where(to_owner, offset, 0), axis=1)
    send_index = jnp.where(lowest < blocks_here, lowest, 0)
    send_index = jnp.stack([send_index, highest], axis=2).reshape(layers, width * capacity)

    side = 8
    half = (POOL - 1) // 2
    blocked = (layers, blocks_here, BLOCK, head_dim)
    key_blocks, value_blocks = keys.reshape(blocked), values.reshape(blocked)
    works = [
        lambda after, done, first=first: pack(
            send_index, key_blocks, value_blocks, first, 2, after, done
        )
        for first in (0, 2)
    ]
    windowed, parcels, arrivals = spread(queries, "ctx", works)
    windowed = windowed.reshape(layers, rows, head_dim)
    start = position * shard_len
    limit = jnp.stack([total_len - window - start, start])
    scale = head_dim**-0.5 * math.log2(math.e)
    parcels = gate(parcels, *arrivals)
    got = lax.all_to_all(parcels, "ctx", split_axis=0, concat_axis=0, tiled=True)

    kept, owner = gate(kept, windowed), gate(owner, windowed)
    source = kept // blocks_here
    entry = jnp.arange(keep_count, dtype=jnp.int32)
    earlier = entry[None, :] < entry[:, None]
    same_owner = owner[:, :, None] == owner[:, None, :]
    same_source = source[:, :, None] == source[:, None, :]
    owner_rank = jnp.sum(same_owner & earlier, axis=-1)
    pair_rank = jnp.sum(same_owner & same_source & earlier, axis=-1)
    recv_hit = (owner == position)[..., None] & (
        owner_rank[..., None] == jnp.arange(keep_share, dtype=jnp.int32)
    )
    recv_index = jnp.sum(jnp.where(recv_hit, (source * capacity + pair_rank)[..., None], 0), axis=1)

    peak, total = local_stats(limit, windowed, keys, group, scale)
    ends = jnp.stack([keys[:, shard_len - side :], keys[:, :side]])
    peak, total, low, high = merge_stats(
        peak.reshape(layers, rows), total.reshape(layers, rows), ends, "ctx"
    )
    low = low.reshape(layers, side, head_dim)
    edges = jnp.concatenate([low, high.reshape(layers, side, head_dim)], axis=1).astype(keys.dtype)
    factor = (total_len / rows) / total
    mass, edge_mass = local_mass(
        limit, windowed, keys, edges, peak[..., None], factor[..., None], group, scale, total_len
    )
    padded = jnp.concatenate(
        [edge_mass[:, 0, side - half : side], mass[:, 0], edge_mass[:, 0, side : side + half]],
        axis=1,
    )
    pooled = padded[:, 0:shard_len]
    for shift in range(1, POOL):
        pooled = pooled + padded[:, shift : shift + shard_len]
    pooled = pooled / POOL
    shared = total_over(pooled, "head") / KVH
    block_mass = jnp.sum(pooled.reshape(layers, blocks_here, BLOCK), axis=2).astype(jnp.bfloat16)
    sent_mass = jnp.take_along_axis(block_mass, send_index, axis=1)
    got, sent_mass = lax.optimization_barrier((got, sent_mass))
    got_mass = lax.all_to_all(sent_mass, "ctx", split_axis=1, concat_axis=1, tiled=True)
    kept_mass = jnp.take_along_axis(got_mass, recv_index, axis=1)

    compact_keys, compact_values = unpack(recv_index, got)
    share = (layers, heads_here, keep_share * BLOCK, head_dim)
    return (
        pooled[:, None],
        shared,
        compact_keys.reshape(share),
        compact_values.reshape(share),
        kept_mass[:, None],
    )


def solution(mesh):
    in_specs = (
        P(None, "ctx", "head", None),
        P(None, "ctx", "head", None),
        P(None, "ctx", "head", None),
        P(None, "head", None),
        P(None, "head", None),
    )
    out_specs = (
        P(None, "head", "ctx"),
        P(None, "ctx"),
        P(None, "head", "ctx", None),
        P(None, "head", "ctx", None),
        P(None, "head", "ctx"),
    )
    return jax.shard_map(
        per_device, mesh=mesh, in_specs=in_specs, out_specs=out_specs, check_vma=False
    )
```

```python
import functools
import math
import jax
import jax.numpy as jnp
from jax import lax
from jax.experimental import pallas as pl
from jax.experimental.pallas import tpu as pltpu
from jax.sharding import PartitionSpec as P

KVH = 8
BLOCK = 128
POOL = 7
LANES = 128
TILE = 1024
NEG = -1e30
MIB = 1 << 20


def pack_kernel(first, parts, index_ref, keys_ref, values_ref, *rest):
    out_ref = rest[-1]
    step = first + pl.program_id(0)
    layer, part = step // parts, step % parts
    share = out_ref.shape[0]
    for slot in range(share):
        block = index_ref[layer, part * share + slot]
        out_ref[slot, 0] = keys_ref[0, block]
        out_ref[slot, 1] = values_ref[0, block]


def pack(index, keys, values, first, count, after, parcels=None):
    layers, slots = index.shape
    parts = 2
    whole = pl.BlockSpec((1,) + keys.shape[1:], lambda i: ((first + i) // parts, 0, 0, 0))
    others = [after] if parcels is None else [after, parcels]
    return pl.pallas_call(
        functools.partial(pack_kernel, first, parts),
        out_shape=jax.ShapeDtypeStruct((slots, 2 * layers) + keys.shape[2:], keys.dtype),
        grid=(count,),
        in_specs=[pl.BlockSpec(memory_space=pltpu.SMEM), whole, whole]
        + [pl.BlockSpec(memory_space=pl.ANY)] * len(others),
        out_specs=pl.BlockSpec(
            (slots // parts, 2) + keys.shape[2:],
            lambda i: ((first + i) % parts, (first + i) // parts, 0, 0),
        ),
        input_output_aliases={} if parcels is None else {4: 0},
        compiler_params=pltpu.CompilerParams(vmem_limit_bytes=60 * MIB),
        cost_estimate=pl.CostEstimate(flops=0, bytes_accessed=8 * MIB, transcendentals=0),
        name="pack",
    )(index, keys, values, *others)


def gate_kernel(*refs):
    pass


def gate(array, *after):
    return pl.pallas_call(
        gate_kernel,
        out_shape=jax.ShapeDtypeStruct(array.shape, array.dtype),
        in_specs=[pl.BlockSpec(memory_space=pl.ANY)] * (1 + len(after)),
        out_specs=pl.BlockSpec(memory_space=pl.ANY),
        input_output_aliases={0: 0},
        name="gate",
    )(array, *after)


def unpack_kernel(index_ref, got_ref, keys_ref, values_ref, sems):
    layers, count = index_ref.shape

    def body(entry, carry):
        for layer in range(layers):
            slot = index_ref[layer, entry]
            pltpu.make_async_copy(
                got_ref.at[slot, 2 * layer], keys_ref.at[layer, entry], sems.at[0]
            ).start()
            pltpu.make_async_copy(
                got_ref.at[slot, 2 * layer + 1], values_ref.at[layer, entry], sems.at[1]
            ).start()
        return carry

    lax.fori_loop(0, count, body, 0)
    pltpu.make_async_copy(keys_ref, keys_ref, sems.at[0]).wait()
    pltpu.make_async_copy(values_ref, values_ref, sems.at[1]).wait()


def unpack(index, got):
    layers, count = index.shape
    out = jax.ShapeDtypeStruct((layers, count) + got.shape[2:], got.dtype)
    return pl.pallas_call(
        unpack_kernel,
        out_shape=(out, out),
        in_specs=[pl.BlockSpec(memory_space=pltpu.SMEM), pl.BlockSpec(memory_space=pl.ANY)],
        out_specs=(pl.BlockSpec(memory_space=pltpu.VMEM), pl.BlockSpec(memory_space=pltpu.VMEM)),
        scratch_shapes=[pltpu.SemaphoreType.DMA((2,))],
        compiler_params=pltpu.CompilerParams(vmem_limit_bytes=60 * MIB),
        cost_estimate=pl.CostEstimate(flops=0, bytes_accessed=4 * MIB, transcendentals=0),
        name="unpack",
    )(index, got)


def logits(limit_ref, query_ref, key_ref, group, scale):
    raw = lax.dot_general(
        query_ref[0], key_ref[0], (((1,), (1,)), ((), ())), preferred_element_type=jnp.float32
    )
    start = pl.program_id(1) * TILE
    row = lax.broadcasted_iota(jnp.int32, raw.shape, 0) // group
    column = lax.broadcasted_iota(jnp.int32, raw.shape, 1) + start
    return jnp.where(column <= row + limit_ref[0], raw * scale, NEG)


def stats_kernel(group, scale, limit_ref, query_ref, key_ref, peak_ref, total_ref, peaks, totals):
    tile = pl.program_id(1)

    @pl.when(tile == 0)
    def _():
        peaks[...] = jnp.full_like(peaks, NEG)
        totals[...] = jnp.zeros_like(totals)

    score = logits(limit_ref, query_ref, key_ref, group, scale)
    rows, width = score.shape
    parts = [score[:, c : c + LANES] for c in range(0, width, LANES)]
    old = peaks[...]
    new = functools.reduce(jnp.maximum, parts, old)
    total = totals[...] * jnp.exp2(old - new)
    for part in parts:
        total = total + jnp.exp2(part - new)
    peaks[...] = new
    totals[...] = total

    @pl.when(tile == pl.num_programs(1) - 1)
    def _():
        peak = jnp.max(new, axis=1, keepdims=True)
        peak_ref[0] = peak
        total_ref[0] = jnp.sum(total * jnp.exp2(new - peak), axis=1, keepdims=True)


def local_stats(limit, query, keys, group, scale):
    layers, rows, head_dim = query.shape
    tiles = keys.shape[1] // TILE
    out = jax.ShapeDtypeStruct((layers, rows, 1), jnp.float32)
    spec = pl.BlockSpec((1, rows, 1), lambda l, t: (l, 0, 0))
    return pl.pallas_call(
        functools.partial(stats_kernel, group, scale),
        out_shape=(out, out),
        grid=(layers, tiles),
        in_specs=[
            pl.BlockSpec(memory_space=pltpu.SMEM),
            pl.BlockSpec((1, rows, head_dim), lambda l, t: (l, 0, 0)),
            pl.BlockSpec((1, TILE, head_dim), lambda l, t: (l, t, 0)),
        ],
        out_specs=(spec, spec),
        scratch_shapes=[pltpu.VMEM((rows, LANES), jnp.float32)] * 2,
        compiler_params=pltpu.CompilerParams(vmem_limit_bytes=60 * MIB),
        cost_estimate=pl.CostEstimate(
            flops=2 * layers * rows * keys.shape[1] * head_dim,
            bytes_accessed=keys.size * 2,
            transcendentals=layers * rows * keys.shape[1],
        ),
        name="stats",
    )(limit, query, keys)


def mass_kernel(
    group, scale, shard_len, total_len, limit_ref, query_ref, key_ref, edge_ref, peak_ref, factor_ref,
    mass_ref, edge_mass_ref,
):
    score = logits(limit_ref, query_ref, key_ref, group, scale)
    weight = jnp.exp2(score - peak_ref[0]) * factor_ref[0]
    mass_ref[0] = jnp.sum(weight, axis=0, keepdims=True)

    @pl.when(pl.program_id(1) == 0)
    def _():
        raw = lax.dot_general(
            query_ref[0],
            edge_ref[0],
            (((1,), (1,)), ((), ())),
            preferred_element_type=jnp.float32,
        )
        side = raw.shape[1] // 2
        row = lax.broadcasted_iota(jnp.int32, raw.shape, 0) // group
        column = lax.broadcasted_iota(jnp.int32, raw.shape, 1)
        column = jnp.where(column < side, column - side, column - side + shard_len)
        start = limit_ref[1]
        inside = (column + start >= 0) & (column + start < total_len)
        inside = inside & (column <= row + limit_ref[0])
        weight = jnp.exp2(jnp.where(inside, raw * scale, NEG) - peak_ref[0]) * factor_ref[0]
        edge_mass_ref[0] = jnp.sum(weight, axis=0, keepdims=True)


def local_mass(limit, query, keys, edges, peak, factor, group, scale, total_len):
    layers, rows, head_dim = query.shape
    shard_len = keys.shape[1]
    tiles = shard_len // TILE
    column = pl.BlockSpec((1, rows, 1), lambda l, t: (l, 0, 0))
    return pl.pallas_call(
        functools.partial(mass_kernel, group, scale, shard_len, total_len),
        out_shape=(
            jax.ShapeDtypeStruct((layers, 1, shard_len), jnp.float32),
            jax.ShapeDtypeStruct((layers, 1, edges.shape[1]), jnp.float32),
        ),
        grid=(layers, tiles),
        in_specs=[
            pl.BlockSpec(memory_space=pltpu.SMEM),
            pl.BlockSpec((1, rows, head_dim), lambda l, t: (l, 0, 0)),
            pl.BlockSpec((1, TILE, head_dim), lambda l, t: (l, t, 0)),
            pl.BlockSpec((1, edges.shape[1], head_dim), lambda l, t: (l, 0, 0)),
            column,
            column,
        ],
        out_specs=(
            pl.BlockSpec((1, 1, TILE), lambda l, t: (l, 0, t)),
            pl.BlockSpec((1, 1, edges.shape[1]), lambda l, t: (l, 0, 0)),
        ),
        compiler_params=pltpu.CompilerParams(vmem_limit_bytes=60 * MIB),
        cost_estimate=pl.CostEstimate(
            flops=2 * layers * rows * shard_len * head_dim,
            bytes_accessed=keys.size * 2,
            transcendentals=layers * rows * shard_len,
        ),
        name="mass",
    )(limit, query, keys, edges, peak, factor)


def grid_of(axis):
    width = lax.axis_size(axis)
    deep = 8 if width % 8 == 0 else width
    return width // deep, deep


def spread(x, axis, works):
    wide, deep = grid_of(axis)
    place = lax.axis_index(axis)
    across, along = place // deep, place % deep
    last = wide * deep - 1
    pieces = x.reshape((wide, -1) + x.shape[2:])
    moved = [
        lax.ppermute(pieces[k], axis, [(last, k * deep + deep - 1)]) for k in range(wide - 1)
    ]
    piece = jnp.where(place == last, pieces[wide - 1], functools.reduce(jnp.add, moved))
    held, result = [deep - 1], None
    for work, steps in zip(works, (range(2, deep, 2), (1,))):
        moved = [
            lax.ppermute(
                piece,
                axis,
                [(k * deep + z, k * deep + (z + dz) % deep) for k in range(wide) for z in held],
            )
            for dz in steps
        ]
        result = work(piece, result)
        mine = functools.reduce(jnp.logical_or, [along == z for z in held])
        piece = jnp.where(mine, piece, functools.reduce(jnp.add, moved))
        piece = gate(piece, result)
        held = held + [(z + dz) % deep for z in held for dz in steps]
    moved = [piece] + [
        lax.ppermute(
            piece,
            axis,
            [(k * deep + z, (k + dx) % wide * deep + z) for k in range(wide) for z in range(deep)],
        )
        for dx in range(1, wide)
    ]
    whole = [lax.select_n((across - k) % wide, *moved) for k in range(wide)]
    return jnp.stack(whole).reshape(x.shape), result, moved[1:]


def partners(axis, bit):
    return [(i, i ^ bit) for i in range(lax.axis_size(axis))]


def merge_stats(peak, total, ends, axis):
    layers, rows = peak.shape
    ends = ends.astype(jnp.float32).reshape(2, -1, rows)
    both = [peak, total, ends[0], ends[1]]
    used = sum(part.shape[0] for part in both)
    both = jnp.concatenate(both + [jnp.zeros((16 - used, rows), jnp.float32)], axis=0)
    every = lax.all_gather(both, axis, axis=0, tiled=False)
    peaks, totals = every[:, :layers], every[:, layers : 2 * layers]
    top = jnp.max(peaks, axis=0)
    total = jnp.sum(totals * jnp.exp2(peaks - top), axis=0)
    place, width = lax.axis_index(axis), lax.axis_size(axis)
    count = ends.shape[1]
    below = lax.dynamic_index_in_dim(every, jnp.maximum(place - 1, 0), 0, keepdims=False)
    above = lax.dynamic_index_in_dim(every, jnp.minimum(place + 1, width - 1), 0, keepdims=False)
    first = 2 * layers
    return top, total, below[first : first + count], above[first + count : first + 2 * count]


def total_over(x, axis):
    bit = 1
    while bit < lax.axis_size(axis):
        x = x + lax.ppermute(x, axis, partners(axis, bit))
        bit *= 2
    return x


def per_device(keys, values, queries, keep_blocks, block_owner):
    width = lax.axis_size("ctx")
    position = lax.axis_index("ctx")
    layers, shard_len, heads_here, head_dim = keys.shape
    window = queries.shape[1]
    group = queries.shape[2] // heads_here
    total_len = shard_len * width
    rows = window * group
    blocks_here = shard_len // BLOCK
    keep_count = keep_blocks.shape[2]
    keep_share = keep_count // width
    capacity = 2
    keys = keys.reshape(layers, shard_len, head_dim)
    values = values.reshape(layers, shard_len, head_dim)
    kept, owner = keep_blocks[:, 0], block_owner[:, 0]
    offset = (kept - position * blocks_here)[..., None]
    to_owner = (offset >= 0) & (offset < blocks_here)
    to_owner = to_owner & (owner[..., None] == jnp.arange(width, dtype=jnp.int32))
    lowest = jnp.min(jnp.where(to_owner, offset, blocks_here), axis=1)
    highest = jnp.max(jnp.where(to_owner, offset, 0), axis=1)
    send_index = jnp.where(lowest < blocks_here, lowest, 0)
    send_index = jnp.stack([send_index, highest], axis=2).reshape(layers, width * capacity)

    side = 8
    half = (POOL - 1) // 2
    blocked = (layers, blocks_here, BLOCK, head_dim)
    key_blocks, value_blocks = keys.reshape(blocked), values.reshape(blocked)
    works = [
        lambda after, done, first=first: pack(
            send_index, key_blocks, value_blocks, first, 2, after, done
        )
        for first in (0, 2)
    ]
    windowed, parcels, arrivals = spread(queries, "ctx", works)
    windowed = windowed.reshape(layers, rows, head_dim)
    start = position * shard_len
    limit = jnp.stack([total_len - window - start, start])
    scale = head_dim**-0.5 * math.log2(math.e)
    parcels = gate(parcels, *arrivals)
    got = lax.all_to_all(parcels, "ctx", split_axis=0, concat_axis=0, tiled=True)

    kept, owner = gate(kept, windowed), gate(owner, windowed)
    source = kept // blocks_here
    entry = jnp.arange(keep_count, dtype=jnp.int32)
    earlier = entry[None, :] < entry[:, None]
    same_owner = owner[:, :, None] == owner[:, None, :]
    same_source = source[:, :, None] == source[:, None, :]
    owner_rank = jnp.sum(same_owner & earlier, axis=-1)
    pair_rank = jnp.sum(same_owner & same_source & earlier, axis=-1)
    recv_hit = (owner == position)[..., None] & (
        owner_rank[..., None] == jnp.arange(keep_share, dtype=jnp.int32)
    )
    recv_index = jnp.sum(jnp.where(recv_hit, (source * capacity + pair_rank)[..., None], 0), axis=1)

    peak, total = local_stats(limit, windowed, keys, group, scale)
    ends = jnp.stack([keys[:, shard_len - side :], keys[:, :side]])
    peak, total, low, high = merge_stats(
        peak.reshape(layers, rows), total.reshape(layers, rows), ends, "ctx"
    )
    low = low.reshape(layers, side, head_dim)
    edges = jnp.concatenate([low, high.reshape(layers, side, head_dim)], axis=1).astype(keys.dtype)
    factor = (total_len / rows) / total
    mass, edge_mass = local_mass(
        limit, windowed, keys, edges, peak[..., None], factor[..., None], group, scale, total_len
    )
    padded = jnp.concatenate(
        [edge_mass[:, 0, side - half : side], mass[:, 0], edge_mass[:, 0, side : side + half]],
        axis=1,
    )
    pooled = padded[:, 0:shard_len]
    for shift in range(1, POOL):
        pooled = pooled + padded[:, shift : shift + shard_len]
    pooled = pooled / POOL
    shared = total_over(pooled, "head") / KVH
    block_mass = jnp.sum(pooled.reshape(layers, blocks_here, BLOCK), axis=2).astype(jnp.bfloat16)
    wide, deep = grid_of("ctx")
    across = position // deep
    sent_mass = jnp.take_along_axis(block_mass, send_index, axis=1).astype(jnp.float32)
    rows_mass = [sent_mass] + [
        lax.ppermute(
            sent_mass,
            "ctx",
            [(k * deep + z, (k + dx) % wide * deep + z) for k in range(wide) for z in range(deep)],
        )
        for dx in range(1, wide)
    ]
    rows_mass = jnp.stack(rows_mass).reshape(wide, layers, wide, deep, capacity)
    mine = jnp.arange(wide, dtype=jnp.int32)[:, None, None] == across
    rows_mass = jnp.sum(jnp.where(mine, rows_mass, 0.0), axis=2)
    rows_mass = gate(rows_mass.reshape(1, -1), shared)

    def from_before(x, dz):
        pairs = [(k * deep + z, k * deep + (z + dz) % deep) for k in range(wide) for z in range(deep)]
        return lax.ppermute(x, "ctx", pairs)

    even = [rows_mass] + [from_before(rows_mass, dz) for dz in range(2, deep, 2)]
    even = jnp.concatenate(even, axis=0)
    got, even = lax.optimization_barrier((got, even))
    got_mass = jnp.stack([even, from_before(even, 1)], axis=1)
    layer = jnp.arange(layers, dtype=jnp.int32)[:, None]
    from_row, from_column = recv_index // capacity % deep, recv_index // capacity // deep
    along = position % deep
    mass_index = (along - from_row) % deep * wide + (across - from_column) % wide
    mass_index = (mass_index * layers + layer) * deep + along
    mass_index = mass_index * capacity + recv_index % capacity
    wanted = mass_index[..., None] == jnp.arange(got_mass.size, dtype=jnp.int32)
    kept_mass = jnp.sum(jnp.where(wanted, got_mass.reshape(-1), 0.0), axis=2).astype(jnp.bfloat16)

    compact_keys, compact_values = unpack(recv_index, got)
    share = (layers, heads_here, keep_share * BLOCK, head_dim)
    return (
        pooled[:, None],
        shared,
        compact_keys.reshape(share),
        compact_values.reshape(share),
        kept_mass[:, None],
    )


def solution(mesh):
    in_specs = (
        P(None, "ctx", "head", None),
        P(None, "ctx", "head", None),
        P(None, "ctx", "head", None),
        P(None, "head", None),
        P(None, "head", None),
    )
    out_specs = (
        P(None, "head", "ctx"),
        P(None, "ctx"),
        P(None, "head", "ctx", None),
        P(None, "head", "ctx", None),
        P(None, "head", "ctx"),
    )
    return jax.shard_map(
        per_device, mesh=mesh, in_specs=in_specs, out_specs=out_specs, check_vma=False
    )
```
